512 devices in a mesh: island: 4 (over y_lo), fsdp: 128 (over x, z, y_hi, core).
Axes of the slice: x: 4, y: 8 (y_hi: 2, y_lo: 4; y = y_hi * 4 + y_lo), z: 8, core: 2. Of those that a mesh axis runs over, the one named last changes fastest.
Arguments:
- tokens: bfloat16 [4, 384, 4096], P('island', 'fsdp'), may hold values from -6 to 6
- cotangent: bfloat16 [4, 384, 4096], P('island', 'fsdp'), may hold values from -0.4375 to 0.4375
- w_gate: bfloat16 [14336, 4096], P('fsdp', 'island'), may hold values from -0.09375 to 0.09375
- w_up: bfloat16 [14336, 4096], P('fsdp', 'island'), may hold values from -0.09375 to 0.09375
- down_master: float32 [4, 14336, 4096], P('island', 'fsdp'), may hold values from -3 to 3
- second_moment: float32 [4, 14336], P('island', 'fsdp'), may hold values from 0.3 to 3
- outer_params: float32 [4194304], P('fsdp'), may hold values from -6 to 6
- inner_params: float32 [4, 4194304], P('island', 'fsdp'), may hold values from -6 to 6
- outer_momentum: float32 [4194304], P('fsdp'), may hold values from -3 to 3
Outputs:
- new_down: float32 [4, 14336, 4096], P('island', 'fsdp')
- new_second: float32 [4, 14336], P('island', 'fsdp')
- new_outer: float32 [4194304], P('fsdp')
- new_momentum: float32 [4194304], P('fsdp')
The draws below stay inside these ranges and needn't reach their ends.
All inputs are finite; a program needn't handle non-finite values.
Results may differ from the reference program's by a relative error of at most 0.0018.
Values may be sent and summed in bfloat16 or wider, within the bound.
No kernel may reach another device: no remote copies, remote signals or barrier semaphores. Data moves between devices by JAX's collectives and lax.ppermute only.
A program may use at most 64 MiB of HBM per device.

```python
import math
import jax
import jax.numpy as jnp
from jax import lax

D = 4096
FW = 14336
ROWS = 384
FRAG = 4194304
N_ISLAND = 4


def level_of(rng, extent, shards, least, top_value):
    factor_of, own = 1.0, jax.random.fold_in(rng, 6)
    for position, blocks in shards:
        draws = jnp.exp(jax.random.uniform(jax.random.fold_in(own, position), (blocks,), jnp.float32, least / len(shards), top_value / len(shards)))
        factor_of = factor_of * jnp.repeat(draws, extent[position] // blocks).reshape([-1 if axis == position else 1 for axis in range(len(extent))])
    return factor_of


def scatter_about(key, shape, scale, reach, pieces=(), kind=jnp.bfloat16):
    level = level_of(key, shape, pieces, -0.22, 0.18) if pieces else 1.0
    array = jax.random.normal(key, shape, jnp.float32) * scale * level
    return jnp.minimum(jnp.maximum(array, -reach), reach).astype(kind)


def setup_inputs(seed: int = 0) -> dict:
    key_list = jax.random.split(jax.random.key(seed), 10)
    tokens = scatter_about(key_list[0], (N_ISLAND, ROWS, D), 1.0, 6.0, ((0, 4), (1, 128)))
    cotangent = scatter_about(key_list[1], (N_ISLAND, ROWS, D), (ROWS // 2) ** -0.5, 0.4375, ((0, 4), (1, 128)))
    w_gate = scatter_about(key_list[2], (FW, D), D ** -0.5, 0.09375, ((0, 128), (1, 4)))
    w_up = scatter_about(key_list[3], (FW, D), D ** -0.5, 0.09375, ((0, 128), (1, 4)))
    down_master = scatter_about(key_list[4], (N_ISLAND, FW, D), 0.5, 3.0, ((0, 4), (1, 128)), jnp.float32)
    second_moment = jnp.clip(jnp.exp(math.log(3.0) - 2.3025851 * jax.random.uniform(key_list[5], (N_ISLAND, FW), jnp.float32) ** level_of(key_list[5], (N_ISLAND, FW), ((0, 4), (1, 128)), -0.2, 0.2)), 0.3, 3.0)
    outer_params = scatter_about(key_list[6], (FRAG,), 1.0, 6.0, ((0, 128),), jnp.float32)
    inner_params = scatter_about(key_list[7], (N_ISLAND, FRAG), 1.0, 6.0, ((0, 4), (1, 128)), jnp.float32)
    outer_momentum = scatter_about(key_list[8], (FRAG,), 0.5, 3.0, ((0, 128),), jnp.float32)
    return {"tokens": tokens, "cotangent": cotangent, "w_gate": w_gate, "w_up": w_up, "down_master": down_master, "second_moment": second_moment, "outer_params": outer_params, "inner_params": inner_params, "outer_momentum": outer_momentum}


def reference(tokens, cotangent, w_gate, w_up, down_master, second_moment, outer_params, inner_params, outer_momentum):
    downs = []
    seconds = []
    contract = (((1,), (1,)), ((), ()))
    rows_pair = (((0,), (0,)), ((), ()))
    for replica in range(N_ISLAND):
        inputs = tokens[replica]
        gate = lax.dot_general(inputs, w_gate, contract, preferred_element_type=jnp.float32)
        upward = lax.dot_general(inputs, w_up, contract, preferred_element_type=jnp.float32)
        hidden = (jax.nn.silu(gate) * upward).astype(jnp.bfloat16)
        grad = lax.dot_general(hidden, cotangent[replica], rows_pair, preferred_element_type=jnp.float32)
        second = 0.95 * second_moment[replica] + 0.05 * lax.optimization_barrier(jnp.mean(grad * grad, axis=1))
        downs.append(down_master[replica] - 0.3 * grad / (jnp.sqrt(second)[:, None] + 1e-08))
        seconds.append(second)
    pseudo = lax.optimization_barrier(jnp.sum(outer_params[None, :] - inner_params, axis=0)) / N_ISLAND
    new_momentum = 0.9 * outer_momentum + pseudo
    new_outer = outer_params - 0.7 * (pseudo + 0.9 * new_momentum)
    return (jnp.stack(downs), jnp.stack(seconds), new_outer, new_momentum)
```

```python
import functools

import jax
import jax.numpy as jnp
import numpy as np
from jax import lax
from jax.experimental import pallas as pl
from jax.experimental.pallas import tpu as pltpu
from jax.sharding import PartitionSpec as P

NX, NZ = 4, 8
BF = jnp.bfloat16
F32 = jnp.float32
ROWS_BY_ROWS = (((1,), (1,)), ((), ()))


def flat(x, z, h, c):
    return (((x % NX) * NZ + z % NZ) * 2 + h) * 2 + c


def pairs(target):
    return [
        (flat(x, z, h, c), flat(*target(x, z, h, c)))
        for x in range(NX)
        for z in range(NZ)
        for h in range(2)
        for c in range(2)
    ]


SWAP = pairs(lambda x, z, h, c: (x, z, h, 1 - c))
HALF = pairs(lambda x, z, h, c: (x, z, 1 - h, c))
EARLY = (
    pairs(lambda x, z, h, c: (x, z ^ 4, h, c)),
    pairs(lambda x, z, h, c: (x, z ^ 2, h, c) if c else (x ^ 2, z, h, c)),
    pairs(lambda x, z, h, c: (x, z ^ 1, h, c) if c else (x ^ 1, z, h, c)),
)
UP = pairs(lambda x, z, h, c: (x + 1, z, h, c) if c else (x, z + 1, h, c))
DOWN = pairs(lambda x, z, h, c: (x - 1, z, h, c) if c else (x, z - 1, h, c))


def row_tables():
    row = np.arange(96)
    e3, e2, e1, half, core, r = (row // 48, row // 24 % 2, row // 12 % 2, row // 6 % 2, row // 3 % 2, row % 3)
    ring = np.concatenate([np.zeros(96), -np.ones(96), np.ones(96), np.where(row < 48, -2, 2)]).astype(np.int32)
    four = lambda v: np.tile(v, 4).astype(np.int32)
    return ring, four(e3), four(e2), four(e1), four(half), four(core), four(r)


def row_ids(me):
    ring, e3, e2, e1, half, core, r = (jnp.asarray(t) for t in row_tables())
    x, z, h = me // 32, me // 4 % 8, me // 2 % 2
    h = h ^ half
    zt = ((z + ring) & 7) ^ (4 * e1)
    xt = x ^ (2 * e2) ^ e3
    zc = z ^ (4 * e1) ^ (2 * e2) ^ e3
    xc = (x + ring) & 3
    tokens = (((xt * 8 + zt) * 2 + h) * 2 + core) * 3 + r
    cots = (((xc * 8 + zc) * 2 + h) * 2 + (1 - core)) * 3 + r
    return tokens[None, :], cots[:, None]


def block_kernel(core_ref, idt_ref, idc_ref, w_ref, dm_ref, sm_ref, *refs):
    own, oth, (nd_ref, ns_ref, hid) = refs[:4], refs[4:8], refs[8:]

    def body(toks, cots):
        for b, tok in enumerate(toks):
            gate, up = None, None
            for j in range(4):
                piece = tok[:, j * 1024 : (j + 1) * 1024]
                g = lax.dot_general(piece, w_ref[j, 0], ROWS_BY_ROWS, preferred_element_type=F32)
                u = lax.dot_general(piece, w_ref[j, 1], ROWS_BY_ROWS, preferred_element_type=F32)
                gate, up = (g, u) if gate is None else (gate + g, up + u)
            hid[b * 96 : (b + 1) * 96, :] = (gate / (1.0 + jnp.exp(-gate)) * up).astype(BF)
        turned = []
        for b in range(4):
            pick = (idc_ref[b * 96 : (b + 1) * 96, :] == idt_ref[...]).astype(F32).astype(BF)
            turned.append(
                lax.dot_general(hid[...], pick, (((0,), (1,)), ((), ())), preferred_element_type=F32).astype(BF)
            )
        total = jnp.zeros((112, 1), F32)
        step = 512
        for d in range(0, 4096, step):
            grad = None
            for b in range(4):
                part = jnp.dot(turned[b], cots[b][:, d : d + step], preferred_element_type=F32)
                grad = part if grad is None else grad + part
            nd_ref[:, d : d + step] = grad
            total = total + jnp.sum(grad * grad, axis=1, keepdims=True)
        second = 0.95 * sm_ref[...] + 0.05 * (total * (1.0 / 4096.0))
        ns_ref[...] = second
        scale = 0.3 / (jnp.sqrt(second) + 1e-08)
        for d in range(0, 4096, step):
            nd_ref[:, d : d + step] = dm_ref[:, d : d + step] - nd_ref[:, d : d + step] * scale

    @pl.when(core_ref[0] == 0)
    def _():
        body(own, oth)

    @pl.when(core_ref[0] == 1)
    def _():
        body(oth, own)


def local(
    tokens,
    cotangent,
    w_gate,
    w_up,
    down_master,
    second_moment,
    outer_params,
    inner_params,
    outer_momentum,
):
    me = lax.axis_index("fsdp")
    core = me % 2
    move = functools.partial(lax.ppermute, axis_name="fsdp")

    weights = lax.all_gather(jnp.stack([w_gate, w_up]), "island", axis=0, tiled=False)
    difference = outer_params - inner_params[0]
    total = lax.psum(difference, "island")

    tok, cot = tokens.reshape(96, 128), cotangent.reshape(96, 128)
    mine = jnp.where(core == 0, tok, cot)
    give = jnp.where(core == 0, cot, tok)
    data = jnp.concatenate([mine, move(give, perm=SWAP)], axis=0)
    data = jnp.concatenate([data, move(data, perm=HALF)], axis=0)
    data = jnp.concatenate([data, move(data, perm=EARLY[0])], axis=0)
    data = jnp.concatenate([data, move(data, perm=EARLY[1])], axis=0)
    data = data.reshape(48, 4096)
    data = jnp.concatenate([data, move(data, perm=EARLY[2])], axis=0)
    below, above = move(data, perm=UP), move(data, perm=DOWN)
    far = jnp.concatenate([move(below[:48], perm=UP), move(above[48:], perm=DOWN)], axis=0)
    own = (data, below, above, far)
    oth = tuple(move(v, perm=SWAP) for v in own)

    idt, idc = row_ids(me)
    vmem = pl.BlockSpec(memory_space=pltpu.VMEM)
    new_down, new_second = pl.pallas_call(
        block_kernel,
        out_shape=(jax.ShapeDtypeStruct((112, 4096), F32), jax.ShapeDtypeStruct((112, 1), F32)),
        in_specs=[pl.BlockSpec(memory_space=pltpu.SMEM)] + [vmem] * 13,
        out_specs=(vmem, vmem),
        scratch_shapes=[pltpu.VMEM((384, 112), BF)],
        compiler_params=pltpu.CompilerParams(vmem_limit_bytes=40 * 2**20),
        cost_estimate=pl.CostEstimate(flops=1_200_000_000, bytes_accessed=12_000_000, transcendentals=43008),
    )(core[None], idt, idc, weights, down_master[0], second_moment[0][:, None], *own, *oth)

    pseudo = total / lax.axis_size("island")
    new_momentum = 0.9 * outer_momentum + pseudo
    new_outer = outer_params - 0.7 * (pseudo + 0.9 * new_momentum)
    return (new_down[None], new_second[:, 0][None], new_outer, new_momentum)


def solution(mesh):
    placed = (
        P("island", "fsdp", None),
        P("island", "fsdp", None),
        P("fsdp", "island"),
        P("fsdp", "island"),
        P("island", "fsdp", None),
        P("island", "fsdp"),
        P("fsdp"),
        P("island", "fsdp"),
        P("fsdp"),
    )
    return jax.shard_map(
        local,
        mesh=mesh,
        in_specs=placed,
        out_specs=(P("island", "fsdp", None), P("island", "fsdp"), P("fsdp"), P("fsdp")),
        check_vma=False,
    )
```

```python
import functools

import jax
import jax.numpy as jnp
import numpy as np
from jax import lax
from jax.experimental import pallas as pl
from jax.experimental.pallas import tpu as pltpu
from jax.sharding import PartitionSpec as P

NX, NZ = 4, 8
BF = jnp.bfloat16
F32 = jnp.float32
ROWS_BY_ROWS = (((1,), (1,)), ((), ()))


def flat(x, z, h, c):
    return (((x % NX) * NZ + z % NZ) * 2 + h) * 2 + c


def pairs(target):
    return [
        (flat(x, z, h, c), flat(*target(x, z, h, c)))
        for x in range(NX)
        for z in range(NZ)
        for h in range(2)
        for c in range(2)
    ]


SWAP = pairs(lambda x, z, h, c: (x, z, h, 1 - c))
HALF = pairs(lambda x, z, h, c: (x, z, 1 - h, c))
FAR = pairs(lambda x, z, h, c: (x, z ^ 4, h, c))
FIRST = tuple(
    pairs(lambda x, z, h, c, s=s: (x, z + s, h, c) if c else (x + s, z, h, c)) for s in (1, -1, -2)
)
UP = pairs(lambda x, z, h, c: (x + 1, z, h, c) if c else (x, z + 1, h, c))
DOWN = pairs(lambda x, z, h, c: (x - 1, z, h, c) if c else (x, z - 1, h, c))


def row_tables():
    row = np.arange(96)
    early = np.array([0, -1, 1, 2])[row // 24]
    ring = np.concatenate([np.zeros(96), -np.ones(96), np.ones(96), np.where(row < 48, -2, 2)])
    inner = [np.tile(v, 4) for v in (early, row // 12 % 2 * 4, row // 6 % 2, row // 3 % 2, row % 3)]
    return [jnp.asarray(v.astype(np.int32)) for v in (ring, *inner)]


def row_ids(me):
    ring, early, four, half, core, r = row_tables()
    x, z, h = me // 32, me // 4 % 8, me // 2 % 2
    h = h ^ half
    tokens = (((((x + early) & 3) * 8 + (((z + ring) & 7) ^ four)) * 2 + h) * 2 + core) * 3 + r
    cots = (((((x + ring) & 3) * 8 + (((z + early) & 7) ^ four)) * 2 + h) * 2 + (1 - core)) * 3 + r
    return tokens[None, :], cots[:, None]


def block_kernel(core_ref, idt_ref, idc_ref, w_ref, dm_ref, sm_ref, *refs):
    own, oth, (nd_ref, ns_ref, hid) = refs[:4], refs[4:8], refs[8:]

    def body(toks, cots):
        for b, tok in enumerate(toks):
            gate, up = None, None
            for j in range(4):
                piece = tok[:, j * 1024 : (j + 1) * 1024]
                g = lax.dot_general(piece, w_ref[j, 0], ROWS_BY_ROWS, preferred_element_type=F32)
                u = lax.dot_general(piece, w_ref[j, 1], ROWS_BY_ROWS, preferred_element_type=F32)
                gate, up = (g, u) if gate is None else (gate + g, up + u)
            hid[b * 96 : (b + 1) * 96, :] = (gate / (1.0 + jnp.exp(-gate)) * up).astype(BF)
        turned = []
        for b in range(4):
            pick = (idc_ref[b * 96 : (b + 1) * 96, :] == idt_ref[...]).astype(F32).astype(BF)
            turned.append(
                lax.dot_general(hid[...], pick, (((0,), (1,)), ((), ())), preferred_element_type=F32).astype(BF)
            )
        total = jnp.zeros((112, 1), F32)
        step = 512
        for d in range(0, 4096, step):
            grad = None
            for b in range(4):
                part = jnp.dot(turned[b], cots[b][:, d : d + step], preferred_element_type=F32)
                grad = part if grad is None else grad + part
            nd_ref[:, d : d + step] = grad
            total = total + jnp.sum(grad * grad, axis=1, keepdims=True)
        second = 0.95 * sm_ref[...] + 0.05 * (total * (1.0 / 4096.0))
        ns_ref[...] = second
        scale = 0.3 / (jnp.sqrt(second) + 1e-08)
        for d in range(0, 4096, step):
            nd_ref[:, d : d + step] = dm_ref[:, d : d + step] - nd_ref[:, d : d + step] * scale

    @pl.when(core_ref[0] == 0)
    def _():
        body(own, oth)

    @pl.when(core_ref[0] == 1)
    def _():
        body(oth, own)


def local(
    tokens,
    cotangent,
    w_gate,
    w_up,
    down_master,
    second_moment,
    outer_params,
    inner_params,
    outer_momentum,
):
    me = lax.axis_index("fsdp")
    core = me % 2
    move = functools.partial(lax.ppermute, axis_name="fsdp")

    weights = lax.all_gather(jnp.stack([w_gate, w_up]), "island", axis=0, tiled=False)
    difference = outer_params - inner_params[0]
    pair = difference + lax.ppermute(difference, "island", ((0, 1), (1, 0), (2, 3), (3, 2)))
    total = pair + lax.ppermute(pair, "island", ((0, 2), (2, 0), (1, 3), (3, 1)))

    tok, cot = tokens.reshape(96, 128), cotangent.reshape(96, 128)
    mine = jnp.where(core == 0, tok, cot)
    give = jnp.where(core == 0, cot, tok)
    data = jnp.concatenate([mine, move(give, perm=SWAP)], axis=0)
    data = jnp.concatenate([data, move(data, perm=HALF)], axis=0)
    data = jnp.concatenate([data, move(data, perm=FAR)], axis=0) + (total[0] * 0).astype(BF)
    data = data.reshape(24, 4096)
    data = jnp.concatenate([data] + [move(data, perm=p) for p in FIRST], axis=0)
    lo, hi = data[:48], data[48:]
    below_lo, above_hi = move(lo, perm=UP), move(hi, perm=DOWN)
    below_hi, above_lo = move(hi, perm=UP), move(lo, perm=DOWN)
    tie = weights[0, 0, 0, 0] * 0
    far = jnp.concatenate([move(below_lo + tie, perm=UP), move(above_hi + tie, perm=DOWN)], axis=0)
    below = jnp.concatenate([below_lo, below_hi], axis=0)
    above = jnp.concatenate([above_lo, above_hi], axis=0)
    own = (data, below, above, far)
    oth = tuple(move(v, perm=SWAP) for v in own)

    idt, idc = row_ids(me)
    vmem = pl.BlockSpec(memory_space=pltpu.VMEM)
    new_down, new_second = pl.pallas_call(
        block_kernel,
        out_shape=(jax.ShapeDtypeStruct((112, 4096), F32), jax.ShapeDtypeStruct((112, 1), F32)),
        in_specs=[pl.BlockSpec(memory_space=pltpu.SMEM)] + [vmem] * 13,
        out_specs=(vmem, vmem),
        scratch_shapes=[pltpu.VMEM((384, 112), BF)],
        compiler_params=pltpu.CompilerParams(vmem_limit_bytes=40 * 2**20),
        cost_estimate=pl.CostEstimate(flops=1_200_000_000, bytes_accessed=12_000_000, transcendentals=43008),
    )(core[None], idt, idc, weights, down_master[0], second_moment[0][:, None], *own, *oth)

    pseudo = total / lax.axis_size("island")
    new_momentum = 0.9 * outer_momentum + pseudo
    new_outer = outer_params - 0.7 * (pseudo + 0.9 * new_momentum)
    return (new_down[None], new_second[:, 0][None], new_outer, new_momentum)


def solution(mesh):
    placed = (
        P("island", "fsdp", None),
        P("island", "fsdp", None),
        P("fsdp", "island"),
        P("fsdp", "island"),
        P("island", "fsdp", None),
        P("island", "fsdp"),
        P("fsdp"),
        P("island", "fsdp"),
        P("fsdp"),
    )
    return jax.shard_map(
        local,
        mesh=mesh,
        in_specs=placed,
        out_specs=(P("island", "fsdp", None), P("island", "fsdp"), P("fsdp"), P("fsdp")),
        check_vma=False,
    )
```

```python
import functools

import jax
import jax.numpy as jnp
import numpy as np
from jax import lax
from jax.experimental import pallas as pl
from jax.experimental.pallas import tpu as pltpu
from jax.sharding import PartitionSpec as P

NX, NZ = 4, 8
BF = jnp.bfloat16
F32 = jnp.float32
ROWS_BY_ROWS = (((1,), (1,)), ((), ()))


def flat(x, z, h, c):
    return (((x % NX) * NZ + z % NZ) * 2 + h) * 2 + c


def pairs(target):
    return [
        (flat(x, z, h, c), flat(*target(x, z, h, c)))
        for x in range(NX)
        for z in range(NZ)
        for h in range(2)
        for c in range(2)
    ]


SWAP = pairs(lambda x, z, h, c: (x, z, h, 1 - c))
HALF = pairs(lambda x, z, h, c: (x, z, 1 - h, c))
FAR = pairs(lambda x, z, h, c: (x, z ^ 4, h, c))
FIRST = tuple(
    pairs(lambda x, z, h, c, s=s: (x, z + s, h, c) if c else (x + s, z, h, c)) for s in (1, -1, -2)
)
UP = pairs(lambda x, z, h, c: (x + 1, z, h, c) if c else (x, z + 1, h, c))
DOWN = pairs(lambda x, z, h, c: (x - 1, z, h, c) if c else (x, z - 1, h, c))


def row_tables():
    row = np.arange(96)
    early = np.array([0, -1, 1, 2])[row // 24]
    ring = np.concatenate([np.zeros(96), -np.ones(96), np.ones(96), np.where(row < 48, -2, 2)])
    inner = [np.tile(v, 4) for v in (early, row // 12 % 2 * 4, row // 6 % 2, row // 3 % 2, row % 3)]
    return [jnp.asarray(v.astype(np.int32)) for v in (ring, *inner)]


def row_ids(me):
    ring, early, four, half, core, r = row_tables()
    x, z, h = me // 32, me // 4 % 8, me // 2 % 2
    h = h ^ half
    tokens = (((((x + early) & 3) * 8 + (((z + ring) & 7) ^ four)) * 2 + h) * 2 + core) * 3 + r
    cots = (((((x + ring) & 3) * 8 + (((z + early) & 7) ^ four)) * 2 + h) * 2 + (1 - core)) * 3 + r
    return tokens[None, :], cots[:, None]


def fetch(refs, buf, sems, base):
    copies, row = [], 0
    for k, ref in enumerate(refs):
        rows = ref.shape[0]
        copies.append(pltpu.make_async_copy(ref, buf.at[pl.ds(row, rows), :], sems.at[base + k]))
        copies[-1].start()
        row += rows
    return copies


def hidden_rows(tok, w_ref):
    both = None
    for j in range(4):
        part = lax.dot_general(
            tok[:, j * 1024 : (j + 1) * 1024],
            w_ref[j].reshape(224, 1024),
            ROWS_BY_ROWS,
            preferred_element_type=F32,
        )
        both = part if both is None else both + part
    gate, up = both[:, :112], both[:, 112:]
    return (gate / (1.0 + jnp.exp(-gate)) * up).astype(BF)


def early_kernel(core_ref, w_ref, *refs):
    own, oth, (hid_ref, tok, sems) = refs[:3], refs[3:6], refs[6:]
    for which, blocks in enumerate((own, oth)):

        @pl.when(core_ref[0] == which)
        def _(blocks=blocks):
            for copy in fetch(blocks, tok, sems, 0):
                copy.wait()

    hid_ref[...] = hidden_rows(tok, w_ref)


def late_kernel(core_ref, idt_ref, idc_ref, hid_ref, w_ref, dm_ref, sm_ref, *refs):
    own, oth, (nd_ref, ns_ref, hid, tok, cot, sems) = refs[:5], refs[5:10], refs[10:]
    eye = lax.broadcasted_iota(jnp.int32, (112, 112), 0) == lax.broadcasted_iota(jnp.int32, (112, 112), 1)
    for which, (toks, cots) in enumerate(((own, oth), (oth, own))):

        @pl.when(core_ref[0] == which)
        def _(toks=toks, cots=cots):
            first, second = fetch(toks[3:], tok, sems, 0), fetch(cots, cot, sems, 2)
            for copy in first:
                copy.wait()
            hid[...] = hidden_rows(tok, w_ref)
            for copy in second:
                copy.wait()

    rows = jnp.concatenate([hid_ref[...], hid[...]], axis=0)
    pick = (idc_ref[...] == idt_ref[...]).astype(F32).astype(BF)
    turned = lax.dot_general(rows, pick, (((0,), (1,)), ((), ())), preferred_element_type=F32).astype(BF)
    total = jnp.zeros((112, 1), F32)
    step = 512
    for d in range(0, 4096, step):
        grad = jnp.dot(turned, cot[:, d : d + step], preferred_element_type=F32)
        nd_ref[:, d : d + step] = grad
        total = total + jnp.sum(grad * grad, axis=1, keepdims=True)
    before = jnp.sum(jnp.where(eye, sm_ref[...], 0.0), axis=1, keepdims=True)
    second = 0.95 * before + 0.05 * (total * (1.0 / 4096.0))
    ns_ref[...] = jnp.sum(jnp.where(eye, second, 0.0), axis=0, keepdims=True)
    scale = 0.3 / (jnp.sqrt(second) + 1e-08)
    for d in range(0, 4096, step):
        nd_ref[:, d : d + step] = dm_ref[:, d : d + step] - nd_ref[:, d : d + step] * scale


def local(
    tokens,
    cotangent,
    w_gate,
    w_up,
    down_master,
    second_moment,
    outer_params,
    inner_params,
    outer_momentum,
):
    me = lax.axis_index("fsdp")
    core = me % 2
    move = functools.partial(lax.ppermute, axis_name="fsdp")

    weights = lax.all_gather(jnp.stack([w_gate, w_up]), "island", axis=0, tiled=False)
    tok, cot = tokens.reshape(96, 128), cotangent.reshape(96, 128)
    mine = jnp.where(core == 0, tok, cot)
    give = jnp.where(core == 0, cot, tok)
    came = move(give, perm=SWAP)
    data = jnp.concatenate([mine, came], axis=0)
    difference = outer_params - inner_params[0]
    pair = difference + lax.ppermute(difference, "island", ((0, 1), (1, 0), (2, 3), (3, 2)))
    total = pair + lax.ppermute(pair, "island", ((0, 2), (2, 0), (1, 3), (3, 1)))
    data = jnp.concatenate([data, move(data, perm=HALF)], axis=0)
    data = jnp.concatenate([data, move(data, perm=FAR)], axis=0) + (total[0] * 0).astype(BF)
    data = data.reshape(24, 4096)
    data = jnp.concatenate([data] + [move(data, perm=p) for p in FIRST], axis=0)
    tie = weights[0, 0, 0, 0] * 0
    below, above = move(data, perm=UP), move(data, perm=DOWN)
    far_lo, far_hi = move(below[:48], perm=UP), move(above[48:] + tie, perm=DOWN)
    own = (data, below, above, far_lo, far_hi)
    oth = tuple(move(v, perm=SWAP) for v in own)

    idt, idc = row_ids(me)
    vmem = pl.BlockSpec(memory_space=pltpu.VMEM)
    smem = pl.BlockSpec(memory_space=pltpu.SMEM)
    anywhere = pl.BlockSpec(memory_space=pl.ANY)
    params = pltpu.CompilerParams(vmem_limit_bytes=20 * 2**20)
    hid = pl.pallas_call(
        early_kernel,
        out_shape=jax.ShapeDtypeStruct((288, 112), BF),
        in_specs=[smem, vmem] + [anywhere] * 6,
        out_specs=vmem,
        scratch_shapes=[pltpu.VMEM((288, 4096), BF), pltpu.SemaphoreType.DMA((3,))],
        compiler_params=params,
        cost_estimate=pl.CostEstimate(flops=530_000_000, bytes_accessed=6_500_000, transcendentals=32256),
    )(core[None], weights, *own[:3], *oth[:3])
    new_down, new_second = pl.pallas_call(
        late_kernel,
        out_shape=(jax.ShapeDtypeStruct((112, 4096), F32), jax.ShapeDtypeStruct((1, 112), F32)),
        in_specs=[smem] + [vmem] * 6 + [anywhere] * 10,
        out_specs=(vmem, vmem),
        scratch_shapes=[
            pltpu.VMEM((96, 112), BF),
            pltpu.VMEM((96, 4096), BF),
            pltpu.VMEM((384, 4096), BF),
            pltpu.SemaphoreType.DMA((7,)),
        ],
        compiler_params=params,
        cost_estimate=pl.CostEstimate(flops=530_000_000, bytes_accessed=9_000_000, transcendentals=10752),
    )(core[None], idt, idc, hid, weights, down_master[0], second_moment, *own, *oth)

    pseudo = total / lax.axis_size("island")
    new_momentum = 0.9 * outer_momentum + pseudo
    new_outer = outer_params - 0.7 * (pseudo + 0.9 * new_momentum)
    return (new_down[None], new_second, new_outer, new_momentum)


def solution(mesh):
    placed = (
        P("island", "fsdp", None),
        P("island", "fsdp", None),
        P("fsdp", "island"),
        P("fsdp", "island"),
        P("island", "fsdp", None),
        P("island", "fsdp"),
        P("fsdp"),
        P("island", "fsdp"),
        P("fsdp"),
    )
    return jax.shard_map(
        local,
        mesh=mesh,
        in_specs=placed,
        out_specs=(P("island", "fsdp", None), P("island", "fsdp"), P("fsdp"), P("fsdp")),
        check_vma=False,
    )
```

```python
import functools

import jax
import jax.numpy as jnp
import numpy as np
from jax import lax
from jax.experimental import pallas as pl
from jax.experimental.pallas import tpu as pltpu
from jax.sharding import PartitionSpec as P

NX, NZ = 4, 8
BF = jnp.bfloat16
F32 = jnp.float32
ROWS_BY_ROWS = (((1,), (1,)), ((), ()))


def flat(x, z, h, c):
    return (((x % NX) * NZ + z % NZ) * 2 + h) * 2 + c


def pairs(target):
    return [
        (flat(x, z, h, c), flat(*target(x, z, h, c)))
        for x in range(NX)
        for z in range(NZ)
        for h in range(2)
        for c in range(2)
    ]


SWAP = pairs(lambda x, z, h, c: (x, z, h, 1 - c))
HALF = pairs(lambda x, z, h, c: (x, z, 1 - h, c))
FAR = pairs(lambda x, z, h, c: (x, z ^ 4, h, c))
FIRST = tuple(
    pairs(lambda x, z, h, c, s=s: (x, z + s, h, c) if c else (x + s, z, h, c)) for s in (1, -1, -2)
)
UP = pairs(lambda x, z, h, c: (x + 1, z, h, c) if c else (x, z + 1, h, c))
DOWN = pairs(lambda x, z, h, c: (x - 1, z, h, c) if c else (x, z - 1, h, c))


def row_tables():
    row = np.arange(96)
    early = np.array([0, -1, 1, 2])[row // 24]
    ring = np.concatenate([np.zeros(96), -np.ones(96), np.ones(96), np.where(row < 48, -2, 2)])
    inner = [np.tile(v, 4) for v in (early, row // 12 % 2 * 4, row // 6 % 2, row // 3 % 2, row % 3)]
    return [jnp.asarray(v.astype(np.int32)) for v in (ring, *inner)]


def row_ids(me):
    ring, early, four, half, core, r = row_tables()
    x, z, h = me // 32, me // 4 % 8, me // 2 % 2
    h = h ^ half
    tokens = (((((x + early) & 3) * 8 + (((z + ring) & 7) ^ four)) * 2 + h) * 2 + core) * 3 + r
    cots = (((((x + ring) & 3) * 8 + (((z + early) & 7) ^ four)) * 2 + h) * 2 + (1 - core)) * 3 + r
    return tokens[None, :], cots[:, None]


def fetch(refs, buf, sems, base):
    copies, row = [], 0
    for k, ref in enumerate(refs):
        rows = ref.shape[0]
        copies.append(pltpu.make_async_copy(ref, buf.at[pl.ds(row, rows), :], sems.at[base + k]))
        copies[-1].start()
        row += rows
    return copies


def hidden_rows(tok, w_ref):
    both = None
    for j in range(4):
        part = lax.dot_general(
            tok[:, j * 1024 : (j + 1) * 1024],
            w_ref[j].reshape(224, 1024),
            ROWS_BY_ROWS,
            preferred_element_type=F32,
        )
        both = part if both is None else both + part
    gate, up = both[:, :112], both[:, 112:]
    return (gate / (1.0 + jnp.exp(-gate)) * up).astype(BF)


def keep_kernel(w_hbm, w_ref, zero_ref, sem):
    copy = pltpu.make_async_copy(w_hbm, w_ref, sem)
    copy.start()
    copy.wait()
    zero_ref[...] = w_ref[0, 0, :16, :128] * 0


def early_kernel(core_ref, w_ref, *refs):
    own, oth, (hid_ref, tok, sems) = refs[:3], refs[3:6], refs[6:]
    for which, blocks in enumerate((own, oth)):

        @pl.when(core_ref[0] == which)
        def _(blocks=blocks):
            for copy in fetch(blocks, tok, sems, 0):
                copy.wait()

    hid_ref[...] = hidden_rows(tok, w_ref)


def late_kernel(core_ref, idt_ref, idc_ref, hid_ref, w_ref, dm_ref, sm_ref, *refs):
    own, oth, (nd_ref, ns_ref, hid, tok, cot, sems) = refs[:5], refs[5:10], refs[10:]
    eye = lax.broadcasted_iota(jnp.int32, (112, 112), 0) == lax.broadcasted_iota(jnp.int32, (112, 112), 1)
    for which, (toks, cots) in enumerate(((own, oth), (oth, own))):

        @pl.when(core_ref[0] == which)
        def _(toks=toks, cots=cots):
            first, second = fetch(toks[3:], tok, sems, 0), fetch(cots, cot, sems, 2)
            for copy in first:
                copy.wait()
            hid[...] = hidden_rows(tok, w_ref)
            for copy in second:
                copy.wait()

    rows = jnp.concatenate([hid_ref[...], hid[...]], axis=0)
    pick = (idc_ref[...] == idt_ref[...]).astype(F32).astype(BF)
    turned = lax.dot_general(rows, pick, (((0,), (1,)), ((), ())), preferred_element_type=F32).astype(BF)
    total = jnp.zeros((112, 1), F32)
    step = 512
    for d in range(0, 4096, step):
        grad = jnp.dot(turned, cot[:, d : d + step], preferred_element_type=F32)
        nd_ref[:, d : d + step] = grad
        total = total + jnp.sum(grad * grad, axis=1, keepdims=True)
    before = jnp.sum(jnp.where(eye, sm_ref[...], 0.0), axis=1, keepdims=True)
    second = 0.95 * before + 0.05 * (total * (1.0 / 4096.0))
    ns_ref[...] = jnp.sum(jnp.where(eye, second, 0.0), axis=0, keepdims=True)
    scale = 0.3 / (jnp.sqrt(second) + 1e-08)
    for d in range(0, 4096, step):
        nd_ref[:, d : d + step] = dm_ref[:, d : d + step] - nd_ref[:, d : d + step] * scale


def local(
    tokens,
    cotangent,
    w_gate,
    w_up,
    down_master,
    second_moment,
    outer_params,
    inner_params,
    outer_momentum,
):
    me = lax.axis_index("fsdp")
    core = me % 2
    move = functools.partial(lax.ppermute, axis_name="fsdp")

    weights = lax.all_gather(jnp.stack([w_gate, w_up]), "island", axis=0, tiled=False)
    tok, cot = tokens.reshape(96, 128), cotangent.reshape(96, 128)
    mine = jnp.where(core == 0, tok, cot)
    give = jnp.where(core == 0, cot, tok)
    came = move(give, perm=SWAP)
    data = jnp.concatenate([mine, came], axis=0)
    difference = outer_params - inner_params[0]
    pair = difference + lax.ppermute(difference, "island", ((0, 1), (1, 0), (2, 3), (3, 2)))
    total = pair + lax.ppermute(pair, "island", ((0, 2), (2, 0), (1, 3), (3, 1)))
    data = jnp.concatenate([data, move(data, perm=HALF)], axis=0)
    data = jnp.concatenate([data, move(data, perm=FAR)], axis=0) + (total[0] * 0).astype(BF)
    data = data.reshape(24, 4096)
    data = jnp.concatenate([data] + [move(data, perm=p) for p in FIRST], axis=0)
    vmem = pl.BlockSpec(memory_space=pltpu.VMEM)
    anywhere = pl.BlockSpec(memory_space=pl.ANY)
    weights, zero = pl.pallas_call(
        keep_kernel,
        out_shape=(jax.ShapeDtypeStruct((4, 2, 112, 1024), BF), jax.ShapeDtypeStruct((16, 128), BF)),
        in_specs=[anywhere],
        out_specs=(vmem, vmem),
        scratch_shapes=[pltpu.SemaphoreType.DMA],
        compiler_params=pltpu.CompilerParams(vmem_limit_bytes=8 * 2**20),
        cost_estimate=pl.CostEstimate(flops=2048, bytes_accessed=3_700_000, transcendentals=0),
    )(weights)
    tie = zero[0, 0]
    below, above = move(data, perm=UP), move(data, perm=DOWN)
    far_lo, far_hi = move(below[:48], perm=UP), move(above[48:] + tie, perm=DOWN)
    own = (data, below, above, far_lo, far_hi)
    oth = tuple(move(v, perm=SWAP) for v in own)

    idt, idc = row_ids(me)
    smem = pl.BlockSpec(memory_space=pltpu.SMEM)
    params = pltpu.CompilerParams(vmem_limit_bytes=20 * 2**20)
    hid = pl.pallas_call(
        early_kernel,
        out_shape=jax.ShapeDtypeStruct((288, 112), BF),
        in_specs=[smem, vmem] + [anywhere] * 6,
        out_specs=vmem,
        scratch_shapes=[pltpu.VMEM((288, 4096), BF), pltpu.SemaphoreType.DMA((3,))],
        compiler_params=params,
        cost_estimate=pl.CostEstimate(flops=530_000_000, bytes_accessed=6_500_000, transcendentals=32256),
    )(core[None], weights, *own[:3], *oth[:3])
    new_down, new_second = pl.pallas_call(
        late_kernel,
        out_shape=(jax.ShapeDtypeStruct((112, 4096), F32), jax.ShapeDtypeStruct((1, 112), F32)),
        in_specs=[smem] + [vmem] * 6 + [anywhere] * 10,
        out_specs=(vmem, vmem),
        scratch_shapes=[
            pltpu.VMEM((96, 112), BF),
            pltpu.VMEM((96, 4096), BF),
            pltpu.VMEM((384, 4096), BF),
            pltpu.SemaphoreType.DMA((7,)),
        ],
        compiler_params=params,
        cost_estimate=pl.CostEstimate(flops=530_000_000, bytes_accessed=9_000_000, transcendentals=10752),
    )(core[None], idt, idc, hid, weights, down_master[0], second_moment, *own, *oth)

    pseudo = total / lax.axis_size("island")
    new_momentum = 0.9 * outer_momentum + pseudo
    new_outer = outer_params - 0.7 * (pseudo + 0.9 * new_momentum)
    return (new_down[None], new_second, new_outer, new_momentum)


def solution(mesh):
    placed = (
        P("island", "fsdp", None),
        P("island", "fsdp", None),
        P("fsdp", "island"),
        P("fsdp", "island"),
        P("island", "fsdp", None),
        P("island", "fsdp"),
        P("fsdp"),
        P("island", "fsdp"),
        P("fsdp"),
    )
    return jax.shard_map(
        local,
        mesh=mesh,
        in_specs=placed,
        out_specs=(P("island", "fsdp", None), P("island", "fsdp"), P("fsdp"), P("fsdp")),
        check_vma=False,
    )
```
